32 devices in a mesh: band: 2 (over y), lon: 4 (over z), lat: 2 (over x), lev: 2 (over core).
Axes of the slice: x: 2, y: 2, z: 4, core: 2. Of those that a mesh axis runs over, the one named last changes fastest.
Arguments:
- tracers: float32 [2, 128, 32, 512], P(None, 'lev', 'lon', ('band', 'lat')), parts along dimension 3, may hold values from -6 to 6
- winds: float32 [2, 128, 32, 512], P(None, 'lev', 'lon', ('band', 'lat')), parts along dimension 3, may hold values from -0.24 to 0.24
- surface_class: int32 [4, 32, 1], P(('band', 'lat'), 'lon'), parts along dimension 0, may hold values from 0 to 3; in each aligned block of 8 rows (0 to 7, 8 to 15, ..., all dimensions but the last counted through in order) at most 4 rows name the same one
- w_in: bfloat16 [4, 256, 1024], P('lon', None, 'lev'), may hold values from -0.375 to 0.375
- b_in: bfloat16 [4, 1024], P('lon', 'lev'), may hold values from -4 to 4
- w_out: bfloat16 [4, 1024, 256], P('lon', 'lev'), may hold values from -0.1875 to 0.1875
- b_out: bfloat16 [4, 256], P('lon', 'lev'), may hold values from -3 to 3
Outputs:
- new_state: float32 [2, 128, 32, 512], P(None, 'lev', 'lon', ('band', 'lat')), parts along dimension 3
The draws below stay inside these ranges and needn't reach their ends.
There are 2 independent parts, one for each index of `band`. The reference program is written for one: setup_inputs(seed, part) draws one part's arguments, and reference() takes and returns one part's arrays. A program takes and returns all parts, laid end to end along the dimension named above; an argument that names none is the same for every part. Nothing has to cross between parts.
Inputs may be any that keep to these rules, and one draw needn't show every extreme that they name: `surface_class`: within the 8 blocks of one tile no class is named more than 4 times; some class reaches 4 in some tiles.
All inputs are finite; a program needn't handle non-finite values.
Results may differ from the reference program's by a relative error of at most 0.0095.
Values may be sent and summed in bfloat16 or wider, within the bound.
A program may use at most 64 MiB of HBM per device.

```python
import math
import jax
import jax.numpy as jnp
import numpy as np
from jax import lax

FIELDS = 2
NLEV = 128
HID = 1024
CLON = 8
CLAT = 128
NSUB = 2
NLON = 32
NLAT = 256
LEVB = 64
NF = 256
CLASSES = 4
CAP = 4
N_LEV = 2


def shard_levels(own_key, dims, split, smallest, high):
    gain, own = 1.0, jax.random.fold_in(own_key, 6)
    for dim, shards_of in split:
        steps = jnp.exp(jax.random.uniform(jax.random.fold_in(own, dim), (shards_of,), jnp.float32, smallest / len(split), high / len(split)))
        gain = gain * jnp.repeat(steps, dims[dim] // shards_of).reshape([-1 if axis == dim else 1 for axis in range(len(dims))])
    return gain


def assign_block(key, own, number, rows, number_of, top, most, skew):
    ranking = jax.random.permutation(key, number_of)
    heavy_load, ordinary = shares(number_of, rows * top, most, skew, True), shares(number_of, rows * top, most, skew, False)
    places = jnp.arange(number_of)

    def named(tallies, turn):
        used = int((tallies > 0).sum())
        fixed = max(1, used // 4)
        moved = fixed + (places - fixed + turn * (used - fixed)) % max(1, number_of - fixed)
        return jnp.zeros((number_of,), jnp.int32).at[ranking[jnp.where(places < fixed, places, moved)]].set(jnp.asarray(tallies, jnp.int32))

    tallies = jnp.where(number % 4 == 0, named(heavy_load, number // 4), named(ordinary, number - number // 4 - 1))
    mixed = jax.random.permutation(jax.random.fold_in(own, 3), number_of)
    donor, sink = mixed[0:number_of // 2 * 2:2], mixed[1:number_of // 2 * 2:2]
    slack = jnp.minimum(tallies[donor] - 1, most - tallies[sink]) // 2
    slack = jnp.where((donor == ranking[0]) | (sink == ranking[0]) | (tallies[sink] == 0), 0, jnp.maximum(slack, 0))
    moved = jax.random.randint(jax.random.fold_in(own, 4), (number_of // 2,), 0, 1 << 20) % (slack + 1)
    tallies = tallies.at[donor].add(-moved).at[sink].add(moved)
    items = jnp.searchsorted(jnp.cumsum(tallies), jnp.arange(rows * top), side="right").astype(jnp.int32)
    listing = items.reshape(top, rows).T
    listing = listing[jax.random.permutation(jax.random.fold_in(own, 1), rows)]
    turn = jax.random.randint(jax.random.fold_in(own, 2), (rows, 1), 0, top)
    return jnp.take_along_axis(listing, (jnp.arange(top)[None, :] + turn) % top, axis=1)


def shares(number_of, total, reach, lean, full):
    portions = [(1 << 20) // math.isqrt(standing ** lean) + 1 for standing in range(1, number_of + 1)]
    largest = reach if full else min(reach, max(-(-total // number_of), total * portions[0] // sum(portions)))
    least = 1 if total - largest >= number_of - 1 else 0
    counts, spare = [largest] + [least] * (number_of - 1), total - largest - least * (number_of - 1)
    while spare > 0:
        free = [i for i in range(1, number_of) if counts[i] < largest] or [i for i in range(1, number_of) if counts[i] < reach]
        whole, budget = sum([portions[i] for i in free]), spare
        for i in free:
            more = min(reach - counts[i], max(1, budget * portions[i] // whole), spare)
            counts[i] = counts[i] + more
            spare = spare - more
    return np.array(counts)


def gaussian(own_key, extent, deviation, bound, split=(), kind=jnp.bfloat16):
    entries = deviation * jax.random.normal(own_key, extent, jnp.float32)
    if split:
        entries = entries * shard_levels(own_key, extent, split, -0.22, 0.18)
    return jnp.clip(entries, -bound, bound).astype(kind)


def setup_inputs(seed: int = 0, part: int = 0) -> dict:
    key_list = jax.random.split(jax.random.key(seed), 8)
    part_splits = jax.random.split(jax.random.fold_in(key_list[7], part), 8)
    tracers = gaussian(part_splits[0], (FIELDS, NLEV, NLON, NLAT), 1.0, 6.0, ((1, 2), (2, 4), (3, 2)), jnp.float32)
    winds = jnp.clip(jax.random.uniform(part_splits[1], (2, NLEV, NLON, NLAT), jnp.float32, -0.24, 0.24) * shard_levels(part_splits[1], (2, NLEV, NLON, NLAT), ((1, 2), (2, 4), (3, 2)), -0.4, 0.0), -0.24, 0.24)
    surface_class_keys = jax.random.split(jax.random.fold_in(part_splits[2], 1), (NLAT // CLAT) * NLON // CLON)
    surface_class_turns = jax.random.permutation(jax.random.fold_in(part_splits[2], 3), (NLAT // CLAT) * NLON // CLON)
    surface_class = jax.vmap(lambda own, number: assign_block(jax.random.fold_in(part_splits[2], 2), own, number, CLON, CLASSES, 1, CAP, 2))(surface_class_keys, surface_class_turns).reshape((NLAT // CLAT, NLON, 1))
    w_in = gaussian(key_list[3], (CLASSES, NF, HID), NF ** -0.5, 0.375, ((0, 4), (2, 2)))
    b_in = gaussian(key_list[4], (CLASSES, HID), 1.0, 4.0, ((0, 4), (1, 2)))
    w_out = gaussian(key_list[5], (CLASSES, HID, NF), HID ** -0.5, 0.1875, ((0, 4), (1, 2)))
    b_out = gaussian(key_list[6], (CLASSES, NF), 0.5, 3.0, ((0, 4), (1, 2)))
    return dict(tracers=tracers, winds=winds, surface_class=surface_class, w_in=w_in, b_in=b_in, w_out=w_out, b_out=b_out)


def advance(field, wind):
    east = 0.5 * (wind[0, :, :-1, :] + wind[0, :, 1:, :])
    flux_x = jnp.maximum(east, 0.0) * field[:, :, :-1, :] + jnp.minimum(east, 0.0) * field[:, :, 1:, :]
    north = 0.5 * (wind[1, :, :, :-1] + wind[1, :, :, 1:])
    flux_y = jnp.maximum(north, 0.0) * field[:, :, :, :-1] + jnp.minimum(north, 0.0) * field[:, :, :, 1:]
    div_x = flux_x[:, :, 1:, 1:-1] - flux_x[:, :, :-1, 1:-1]
    div_y = flux_y[:, :, 1:-1, 1:] - flux_y[:, :, 1:-1, :-1]
    return field[:, :, 1:-1, 1:-1] - div_x - div_y


def widen(field):
    looped = jnp.pad(field, ((0, 0), (0, 0), (1, 1), (0, 0)), mode="wrap")
    return jnp.pad(looped, ((0, 0), (0, 0), (0, 0), (1, 1)))


def reference(tracers, winds, surface_class, w_in, b_in, w_out, b_out):
    wind_ext = widen(winds)
    state = tracers
    for step in range(NSUB):
        state = advance(widen(state), wind_ext)
    inputs_all = state.astype(jnp.bfloat16)
    tiles = NLAT // CLAT
    half = HID // N_LEV

    def one_block(index):
        tile = index // NLON
        column = index % NLON
        zero = jnp.zeros((), jnp.int32)
        piece = lax.dynamic_slice(inputs_all, (zero, zero, column.astype(jnp.int32), (tile * CLAT).astype(jnp.int32)), (FIELDS, NLEV, 1, CLAT))
        inputs = piece.reshape(FIELDS, N_LEV, LEVB, CLAT).transpose(3, 1, 0, 2).reshape(CLAT, NF)
        klass = surface_class[tile, column, 0]
        first = w_in[klass]
        second = w_out[klass]
        pre = jnp.dot(inputs, first, preferred_element_type=jnp.float32) + b_in[klass].astype(jnp.float32)
        hidden = jax.nn.silu(pre).astype(jnp.bfloat16)
        total = jnp.zeros((CLAT, NF), jnp.float32)
        for group in range(N_LEV):
            part = jnp.dot(hidden[:, group * half:(group + 1) * half], second[group * half:(group + 1) * half], preferred_element_type=jnp.float32)
            part = lax.optimization_barrier(part.astype(jnp.bfloat16)).astype(jnp.float32)
            total = total + part
        return (total + b_out[klass].astype(jnp.float32)).astype(jnp.bfloat16)

    tendency = lax.map(one_block, jnp.arange(tiles * NLON, dtype=jnp.int32))
    tendency = tendency.reshape(tiles, NLON, CLAT, N_LEV, FIELDS, LEVB).transpose(4, 3, 5, 1, 0, 2).reshape(FIELDS, NLEV, NLON, NLAT)
    return state + 0.5 * tendency.astype(jnp.float32)
```

```python
import functools

import jax
import jax.numpy as jnp
from jax import lax
from jax.experimental import pallas as pl
from jax.experimental.pallas import tpu as pltpu
from jax.sharding import PartitionSpec as P

MESH = pl.DeviceIdType.MESH
F32 = jnp.float32
BF16 = jnp.bfloat16


def step(q, west, east, south, north, u_w, u, u_e, v_s, v, v_n):
    levels = u.shape[0]
    face_e = 0.5 * (u + u_e)
    face_w = 0.5 * (u_w + u)
    face_n = 0.5 * (v + v_n)
    face_s = 0.5 * (v_s + v)
    e_pos, e_neg = jnp.maximum(face_e, 0.0), jnp.minimum(face_e, 0.0)
    w_pos, w_neg = jnp.maximum(face_w, 0.0), jnp.minimum(face_w, 0.0)
    n_pos, n_neg = jnp.maximum(face_n, 0.0), jnp.minimum(face_n, 0.0)
    s_pos, s_neg = jnp.maximum(face_s, 0.0), jnp.minimum(face_s, 0.0)
    parts = []
    for f in range(q.shape[0] // levels):
        cut = slice(f * levels, (f + 1) * levels)
        c = q[cut]
        div_x = (e_pos * c + e_neg * east[cut]) - (w_pos * west[cut] + w_neg * c)
        div_y = (n_pos * c + n_neg * north[cut]) - (s_pos * south[cut] + s_neg * c)
        parts.append((c - div_x) - div_y)
    return jnp.concatenate(parts, axis=0)


def kernel(
    sizes,
    tr_ref, wd_ref, sc_ref, wi_ref, bi_ref, wo_ref, bo_ref,
    out_ref,
    hs, hr, pack, rp, tt, q1, h1, st, xbuf, pbuf, rbuf, wi_all, wo_all, bias,
    hs_sem, hr_sem, ps_sem, pr_sem, loc_sem, a_send, a_recv, b_send, b_recv,
    xs_sem, xr_sem, ys_sem, yr_sem,
):
    nband, nlon, nlat = sizes
    b, z, a, l = (lax.axis_index(n) for n in ("band", "lon", "lat", "lev"))
    clon = out_ref.shape[0] // 128
    rows_i = wi_ref.shape[1] // (nband * 2)
    rows_o = wo_ref.shape[1] // (nband * 2)
    p = b * 2 + lax.rem(a, 2)
    pair = a - lax.rem(a, 2)
    has_low, has_high = a > 0, a < nlat - 1

    def lon_at(d):
        return lax.rem(z + d + nlon, nlon)

    def peer_of(k):
        other = lax.rem(p + k, nband * 2)
        return {"band": other // 2, "lat": pair + lax.rem(other, 2)}, other

    barrier = pltpu.get_barrier_semaphore()
    for d in range(1, nlon):
        pl.semaphore_signal(barrier, inc=1, device_id={"lon": lon_at(d)}, device_id_type=MESH)
    for k in range(1, nband * 2):
        pl.semaphore_signal(barrier, inc=1, device_id=peer_of(k)[0], device_id_type=MESH)
    pl.semaphore_signal(barrier, inc=1, device_id={"lev": 1 - l}, device_id_type=MESH)
    for has, da in ((has_low, -1), (has_high, 1)):
        @pl.when(has)
        def _(da=da):
            for d in (-1, 0, 1):
                pl.semaphore_signal(
                    barrier, inc=1, device_id={"lat": a + da, "lon": lon_at(d)}, device_id_type=MESH
                )

    def own(ref, j):
        return ref[pl.ds(j, 128, stride=clon), :]

    for slot, j in enumerate((0, 1, clon - 2, clon - 1)):
        hs[slot, 0] = own(tr_ref, j).astype(BF16)
        hs[slot, 1] = own(wd_ref, j).astype(BF16)
    bias[z, :, : bi_ref.shape[1]] = jnp.broadcast_to(
        bi_ref[...].astype(F32), (16, bi_ref.shape[1])
    ).astype(BF16)
    bias[z, :, bi_ref.shape[1]:] = jnp.broadcast_to(
        bo_ref[...].astype(F32), (16, bo_ref.shape[1])
    ).astype(BF16)

    sides = (a + nlat - 1) // nlat + (2 * nlat - 2 - a) // nlat
    pl.semaphore_wait(barrier, nlon - 1 + nband * 2 - 1 + 1 + 3 * sides)

    halos = []
    for side, d in ((0, 1), (1, -1)):
        first = 2 if d == 1 else 0
        halos.append(pltpu.make_async_remote_copy(
            src_ref=hs.at[pl.ds(first, 2)], dst_ref=hr.at[side],
            send_sem=hs_sem.at[side], recv_sem=hr_sem.at[side],
            device_id={"lon": lon_at(d)}, device_id_type=MESH,
        ))
        halos[-1].start()

    lane = lax.broadcasted_iota(jnp.int32, (128, 128), 1)
    acc = jnp.zeros((128, 128), F32)
    for base, ref in ((0, tr_ref), (32, wd_ref)):
        for j in range(clon):
            x = own(ref, j)
            for g, col in enumerate((0, 1, 126, 127)):
                place = base + g * 8 + j
                acc = jnp.where(lane == place, pltpu.roll(x, (place - col) % 128, 1), acc)
    pack[...] = acc.astype(BF16)

    def pack_copy(side, d):
        return pltpu.make_async_remote_copy(
            src_ref=pack, dst_ref=rp.at[side, 1 - d],
            send_sem=ps_sem.at[side, 1 - d], recv_sem=pr_sem.at[side, 1 - d],
            device_id={"lat": a + (1 if side == 0 else -1), "lon": lon_at(d)}, device_id_type=MESH,
        )

    for has, side in ((has_low, 1), (has_high, 0)):
        @pl.when(has)
        def _(side=side):
            for d in (0, 1, -1):
                pack_copy(side, d).start()

    local = [
        pltpu.make_async_copy(wi_ref.at[0], wi_all.at[z], loc_sem.at[0]),
        pltpu.make_async_copy(wo_ref.at[0], wo_all.at[z], loc_sem.at[1]),
    ]
    cut_i, cut_o = pl.ds(p * rows_i, rows_i), pl.ds(p * rows_o, rows_o)
    firsts = []
    for d in range(1, nlon):
        trio = []
        for kind, (src, dst) in enumerate((
            (wi_ref.at[0, cut_i], wi_all.at[z, cut_i]),
            (wo_ref.at[0, cut_o], wo_all.at[z, cut_o]),
            (bias.at[z], bias.at[z]),
        )):
            trio.append(pltpu.make_async_remote_copy(
                src_ref=src, dst_ref=dst,
                send_sem=a_send.at[kind, d], recv_sem=a_recv.at[kind, d],
                device_id={"lon": lon_at(d)}, device_id_type=MESH,
            ))
            trio[-1].start()
        firsts.append(trio)
    for copy in local:
        copy.start()

    seconds = []

    def forward(d):
        for copy in firsts[d - 1]:
            copy.wait_recv()
        c = lon_at(-d)
        for k in range(1, nband * 2):
            for kind, (buf, cut) in enumerate(((wi_all, cut_i), (wo_all, cut_o))):
                copy = pltpu.make_async_remote_copy(
                    src_ref=buf.at[c, cut], dst_ref=buf.at[c, cut],
                    send_sem=b_send.at[kind, d, k], recv_sem=b_recv.at[kind, d, k],
                    device_id=peer_of(k)[0], device_id_type=MESH,
                )
                copy.start()
                seconds.append(copy)

    for has, side in ((has_low, 0), (has_high, 1)):
        @pl.when(has)
        def _(side=side):
            for d in (-1, 0, 1):
                pltpu.make_async_copy(
                    rp.at[side, 1 + d], rp.at[side, 1 + d], pr_sem.at[side, 1 + d]
                ).wait()

        @pl.when(jnp.logical_not(has))
        def _(side=side):
            rp[side] = jnp.zeros(rp.shape[1:], BF16)

    from_low = lax.rem(lane, 32) >= 16
    for d in range(3):
        tt[d] = jnp.where(from_low, rp[0, d].astype(F32), rp[1, d].astype(F32))

    first, last = lax.rem(lane, 8) == 0, lax.rem(lane, 8) == 7
    near = lax.rem(lane, 32) < 8
    mid = tt[1]
    edge = {
        "c": mid,
        "w": jnp.where(first, pltpu.roll(tt[0], 121, 1), pltpu.roll(mid, 1, 1)),
        "e": jnp.where(last, pltpu.roll(tt[2], 7, 1), pltpu.roll(mid, 127, 1)),
        "s": jnp.where(near, pltpu.roll(acc, 104, 1), pltpu.roll(mid, 8, 1)),
        "n": jnp.where(near, pltpu.roll(mid, 120, 1), pltpu.roll(acc, 24, 1)),
    }
    wind = {key: pltpu.roll(value, 96, 1) for key, value in edge.items()}
    outer = step(
        edge["c"], edge["w"], edge["e"], edge["s"], edge["n"],
        wind["w"][:64], wind["c"][:64], wind["e"][:64],
        wind["s"][64:], wind["c"][64:], wind["n"][64:],
    )
    outside = jnp.where(lane >= 16, a, nlat - 1 - a) > 0
    h1[...] = jnp.where(outside, outer, 0.0)

    def shifted(x, rim, low_lane, high_lane):
        ln = lane[: x.shape[0]]
        south = jnp.where(ln == 0, pltpu.roll(rim, (128 - low_lane) % 128, 1), pltpu.roll(x, 1, 1))
        north = jnp.where(
            ln == 127, pltpu.roll(rim, (127 - high_lane) % 128, 1), pltpu.roll(x, 127, 1)
        )
        return south, north

    def field(r):
        if r < 0:
            return hr[0, 2 + r, 0].astype(F32)
        if r >= clon:
            return hr[1, r - clon, 0].astype(F32)
        return own(tr_ref, r)

    def zonal(r):
        if r < 0:
            return hr[0, 2 + r, 1, :64].astype(F32)
        if r >= clon:
            return hr[1, r - clon, 1, :64].astype(F32)
        return wd_ref[pl.ds(r, 64, stride=clon), :]

    def merid(r):
        if r < 0:
            return hr[0, 2 + r, 1, 64:].astype(F32)
        if r >= clon:
            return hr[1, r - clon, 1, 64:].astype(F32)
        return wd_ref[pl.ds(64 * clon + r, 64, stride=clon), :]

    def rim_of(r):
        return (0, clon - 1) if r < 0 else (2, 0) if r >= clon else (1, r)

    def advance(r, get, rim):
        slot, j = rim_of(r)
        v = merid(r)
        v_s, v_n = shifted(v, tt[slot, 64:, :], 56 + j, 32 + j)
        q = get(r)
        south, north = shifted(q, rim, 24 + j, j)
        return step(
            q, get(r - 1), get(r + 1), south, north,
            zonal(r - 1), zonal(r), zonal(r + 1), v_s, v, v_n,
        )

    inner = list(range(1, clon - 1))
    for r in inner:
        q1[r + 1] = advance(r, field, tt[1])
    for copy in halos:
        copy.wait_recv()
    for r in (-1, 0, clon - 1, clon):
        q1[r + 1] = advance(r, field, tt[rim_of(r)[0]])

    def x_copy(j):
        return pltpu.make_async_remote_copy(
            src_ref=xbuf.at[l, j], dst_ref=xbuf.at[l, j],
            send_sem=xs_sem.at[j], recv_sem=xr_sem.at[j],
            device_id={"lev": 1 - l}, device_id_type=MESH,
        )

    for r in range(clon):
        new = advance(r, lambda k: q1[k + 1], h1[...])
        st[r] = new
        xbuf[l, r] = new.T.astype(BF16)
        x_copy(r).start()

    for d in range(1, nlon):
        forward(d)
    for copy in seconds:
        copy.wait_recv()
    for copy in local:
        copy.wait()

    def y_copy(j):
        return pltpu.make_async_remote_copy(
            src_ref=pbuf.at[j, 1 - l], dst_ref=rbuf.at[j],
            send_sem=ys_sem.at[j], recv_sem=yr_sem.at[j],
            device_id={"lev": 1 - l}, device_id_type=MESH,
        )

    hid = bi_ref.shape[1]

    @pl.loop(0, clon)
    def _(j):
        x_copy(j).wait_recv()
        c = sc_ref[0, j]
        x = jnp.concatenate([xbuf[0, j], xbuf[1, j]], axis=1)
        pre = jnp.dot(x, wi_all[c], preferred_element_type=F32) + bias[c][0:1, :hid].astype(F32)
        hidden = (pre * jax.nn.sigmoid(pre)).astype(BF16)
        part = jnp.dot(hidden, wo_all[c], preferred_element_type=F32).astype(BF16)
        pbuf[j, 0] = part[:, :128]
        pbuf[j, 1] = part[:, 128:]
        y_copy(j).start()

    @pl.loop(0, clon)
    def _(j):
        y_copy(j).wait_recv()
        c = sc_ref[0, j]
        total = pbuf[j, l].astype(F32) + rbuf[j].astype(F32)
        tend = (total + bias[c][0:1, hid:].astype(F32)).astype(BF16).astype(F32)
        out_ref[pl.ds(j, 128, stride=clon), :] = st[j] + 0.5 * tend.T

    for copy in halos:
        copy.wait_send()
    for has, side in ((has_low, 1), (has_high, 0)):
        @pl.when(has)
        def _(side=side):
            for d in (0, 1, -1):
                pack_copy(side, d).wait_send()
    for trio in firsts:
        for copy in trio:
            copy.wait_send()
    for copy in seconds:
        copy.wait_send()

    @pl.loop(0, clon)
    def _(j):
        x_copy(j).wait_send()
        y_copy(j).wait_send()


def shards(sizes, tracers, winds, surface_class, w_in, b_in, w_out, b_out):
    fields, levb, clon, clat = tracers.shape
    nband, nlon, nlat = sizes
    rows = fields * levb
    flat = (rows * clon, clat)
    members = nband * 2
    vmem = pl.BlockSpec(memory_space=pltpu.VMEM)
    smem = pl.BlockSpec(memory_space=pltpu.SMEM)
    anywhere = pl.BlockSpec(memory_space=pl.ANY)
    dma = pltpu.SemaphoreType.DMA
    new = pl.pallas_call(
        functools.partial(kernel, sizes),
        out_shape=jax.ShapeDtypeStruct(flat, F32),
        in_specs=[vmem, vmem, smem, anywhere, vmem, anywhere, vmem],
        out_specs=vmem,
        scratch_shapes=[
            pltpu.VMEM((4, 2, rows, clat), BF16),
            pltpu.VMEM((2, 2, 2, rows, clat), BF16),
            pltpu.VMEM((rows, clat), BF16),
            pltpu.VMEM((2, 3, rows, clat), BF16),
            pltpu.VMEM((3, rows, clat), F32),
            pltpu.VMEM((clon + 2, rows, clat), F32),
            pltpu.VMEM((rows, clat), F32),
            pltpu.VMEM((clon, rows, clat), F32),
            pltpu.VMEM((2, clon, clat, rows), BF16),
            pltpu.VMEM((clon, 2, clat, rows), BF16),
            pltpu.VMEM((clon, clat, rows), BF16),
            pltpu.VMEM((nlon,) + w_in.shape[1:], BF16),
            pltpu.VMEM((nlon,) + w_out.shape[1:], BF16),
            pltpu.VMEM((nlon, 16, b_in.shape[1] + b_out.shape[1]), BF16),
            dma((2,)), dma((2,)), dma((2, 3)), dma((2, 3)), dma((2,)),
            dma((3, nlon)), dma((3, nlon)), dma((2, nlon, members)), dma((2, nlon, members)),
            dma((clon,)), dma((clon,)), dma((clon,)), dma((clon,)),
        ],
        compiler_params=pltpu.CompilerParams(
            collective_id=0, has_side_effects=True, vmem_limit_bytes=48 * 1024 * 1024
        ),
    )(tracers.reshape(flat), winds.reshape(flat), surface_class.reshape(1, clon), w_in, b_in, w_out, b_out)
    return new.reshape(tracers.shape)


def solution(mesh):
    placed = (
        P(None, "lev", "lon", ("band", "lat")),
        P(None, "lev", "lon", ("band", "lat")),
        P(("band", "lat"), "lon", None),
        P("lon", None, "lev"),
        P("lon", "lev"),
        P("lon", "lev", None),
        P("lon", "lev"),
    )
    sizes = tuple(mesh.shape[name] for name in ("band", "lon", "lat"))
    return jax.shard_map(
        functools.partial(shards, sizes),
        mesh=mesh,
        in_specs=placed,
        out_specs=P(None, "lev", "lon", ("band", "lat")),
        check_vma=False,
    )
```

```python
import functools

import jax
import jax.numpy as jnp
from jax import lax
from jax.experimental import pallas as pl
from jax.experimental.pallas import tpu as pltpu
from jax.sharding import PartitionSpec as P

MESH = pl.DeviceIdType.MESH
F32 = jnp.float32
BF16 = jnp.bfloat16


def step(q, west, east, south, north, u_w, u, u_e, v_s, v, v_n):
    levels = u.shape[0]
    face_e = 0.5 * (u + u_e)
    face_w = 0.5 * (u_w + u)
    face_n = 0.5 * (v + v_n)
    face_s = 0.5 * (v_s + v)
    e_pos, e_neg = jnp.maximum(face_e, 0.0), jnp.minimum(face_e, 0.0)
    w_pos, w_neg = jnp.maximum(face_w, 0.0), jnp.minimum(face_w, 0.0)
    n_pos, n_neg = jnp.maximum(face_n, 0.0), jnp.minimum(face_n, 0.0)
    s_pos, s_neg = jnp.maximum(face_s, 0.0), jnp.minimum(face_s, 0.0)
    parts = []
    for f in range(q.shape[0] // levels):
        cut = slice(f * levels, (f + 1) * levels)
        c = q[cut]
        div_x = (e_pos * c + e_neg * east[cut]) - (w_pos * west[cut] + w_neg * c)
        div_y = (n_pos * c + n_neg * north[cut]) - (s_pos * south[cut] + s_neg * c)
        parts.append((c - div_x) - div_y)
    return jnp.concatenate(parts, axis=0)


def kernel(
    sizes,
    tr_hbm, wd_hbm, sc_ref, wi_ref, bi_ref, wo_ref, bo_ref,
    out_ref,
    tr_ref, wd_ref, hs, hr, pack, rp, tt, q1, h1, st, xbuf, pbuf, rbuf, wi_all, wo_all, bias,
    hs_sem, hr_sem, ps_sem, pr_sem, loc_sem, a_send, a_recv, b_send, b_recv,
    xs_sem, xr_sem, ys_sem, yr_sem,
):
    nband, nlon, nlat = sizes
    b, z, a, l = (lax.axis_index(n) for n in ("band", "lon", "lat", "lev"))
    clon = out_ref.shape[0] // 128
    rows_i = wi_ref.shape[1] // (nband * 2)
    rows_o = wo_ref.shape[1] // (nband * 2)
    p = b * 2 + lax.rem(a, 2)
    pair = a - lax.rem(a, 2)
    has_low, has_high = a > 0, a < nlat - 1

    def lon_at(d):
        return lax.rem(z + d + nlon, nlon)

    def peer_of(k):
        other = lax.rem(p + k, nband * 2)
        return {"band": other // 2, "lat": pair + lax.rem(other, 2)}, other

    local = [
        pltpu.make_async_copy(tr_hbm, tr_ref, loc_sem.at[2]),
        pltpu.make_async_copy(wd_hbm, wd_ref, loc_sem.at[3]),
        pltpu.make_async_copy(wi_ref.at[0], wi_all.at[z], loc_sem.at[0]),
        pltpu.make_async_copy(wo_ref.at[0], wo_all.at[z], loc_sem.at[1]),
    ]
    for copy in local:
        copy.start()

    barrier = pltpu.get_barrier_semaphore()
    for d in range(1, nlon):
        pl.semaphore_signal(barrier, inc=1, device_id={"lon": lon_at(d)}, device_id_type=MESH)
    for k in range(1, nband * 2):
        pl.semaphore_signal(barrier, inc=1, device_id=peer_of(k)[0], device_id_type=MESH)
    pl.semaphore_signal(barrier, inc=1, device_id={"lev": 1 - l}, device_id_type=MESH)
    for has, da in ((has_low, -1), (has_high, 1)):
        @pl.when(has)
        def _(da=da):
            for d in (-1, 0, 1):
                pl.semaphore_signal(
                    barrier, inc=1, device_id={"lat": a + da, "lon": lon_at(d)}, device_id_type=MESH
                )

    def own(ref, j):
        return ref[pl.ds(j, 128, stride=clon), :]

    local[0].wait()
    local[1].wait()
    for slot, j in enumerate((0, 1, clon - 2, clon - 1)):
        hs[slot, 0] = own(tr_ref, j).astype(BF16)
        hs[slot, 1] = own(wd_ref, j).astype(BF16)
    bias[z, :, : bi_ref.shape[1]] = jnp.broadcast_to(
        bi_ref[...].astype(F32), (16, bi_ref.shape[1])
    ).astype(BF16)
    bias[z, :, bi_ref.shape[1]:] = jnp.broadcast_to(
        bo_ref[...].astype(F32), (16, bo_ref.shape[1])
    ).astype(BF16)

    sides = (a + nlat - 1) // nlat + (2 * nlat - 2 - a) // nlat
    pl.semaphore_wait(barrier, nlon - 1 + nband * 2 - 1 + 1 + 3 * sides)

    halos = []
    for side, d in ((0, 1), (1, -1)):
        first = 2 if d == 1 else 0
        halos.append(pltpu.make_async_remote_copy(
            src_ref=hs.at[pl.ds(first, 2)], dst_ref=hr.at[side],
            send_sem=hs_sem.at[side], recv_sem=hr_sem.at[side],
            device_id={"lon": lon_at(d)}, device_id_type=MESH,
        ))
        halos[-1].start()

    cut_i, cut_o = pl.ds(p * rows_i, rows_i), pl.ds(p * rows_o, rows_o)
    order = sorted(range(1, nlon), key=lambda d: min(d, nlon - d))
    firsts = []
    for d in order:
        trio = []
        for kind, (src, dst) in enumerate((
            (wi_ref.at[0, cut_i], wi_all.at[z, cut_i]),
            (wo_ref.at[0, cut_o], wo_all.at[z, cut_o]),
            (bias.at[z], bias.at[z]),
        )):
            trio.append(pltpu.make_async_remote_copy(
                src_ref=src, dst_ref=dst,
                send_sem=a_send.at[kind, d], recv_sem=a_recv.at[kind, d],
                device_id={"lon": lon_at(d)}, device_id_type=MESH,
            ))
            trio[-1].start()
        firsts.append((d, trio))

    lane = lax.broadcasted_iota(jnp.int32, (128, 128), 1)
    acc = jnp.zeros((128, 128), F32)
    for base, ref in ((0, tr_ref), (32, wd_ref)):
        for j in range(clon):
            x = own(ref, j)
            for g, col in enumerate((0, 1, 126, 127)):
                place = base + g * 8 + j
                acc = jnp.where(lane == place, pltpu.roll(x, (place - col) % 128, 1), acc)
    pack[...] = acc.astype(BF16)

    def pack_copy(side, d):
        return pltpu.make_async_remote_copy(
            src_ref=pack, dst_ref=rp.at[side, 1 - d],
            send_sem=ps_sem.at[side, 1 - d], recv_sem=pr_sem.at[side, 1 - d],
            device_id={"lat": a + (1 if side == 0 else -1), "lon": lon_at(d)}, device_id_type=MESH,
        )

    for has, side in ((has_low, 1), (has_high, 0)):
        @pl.when(has)
        def _(side=side):
            for d in (0, 1, -1):
                pack_copy(side, d).start()

    seconds = []

    def forward(d, trio):
        for copy in trio:
            copy.wait_recv()
        c = lon_at(-d)
        for k in range(1, nband * 2):
            for kind, (buf, cut) in enumerate(((wi_all, cut_i), (wo_all, cut_o))):
                copy = pltpu.make_async_remote_copy(
                    src_ref=buf.at[c, cut], dst_ref=buf.at[c, cut],
                    send_sem=b_send.at[kind, d, k], recv_sem=b_recv.at[kind, d, k],
                    device_id=peer_of(k)[0], device_id_type=MESH,
                )
                copy.start()
                seconds.append(copy)

    def shifted(x, rim, low_lane, high_lane):
        ln = lane[: x.shape[0]]
        south = jnp.where(ln == 0, pltpu.roll(rim, (128 - low_lane) % 128, 1), pltpu.roll(x, 1, 1))
        north = jnp.where(
            ln == 127, pltpu.roll(rim, (127 - high_lane) % 128, 1), pltpu.roll(x, 127, 1)
        )
        return south, north

    def field(r):
        if r < 0:
            return hr[0, 2 + r, 0].astype(F32)
        if r >= clon:
            return hr[1, r - clon, 0].astype(F32)
        return own(tr_ref, r)

    def zonal(r):
        if r < 0:
            return hr[0, 2 + r, 1, :64].astype(F32)
        if r >= clon:
            return hr[1, r - clon, 1, :64].astype(F32)
        return wd_ref[pl.ds(r, 64, stride=clon), :]

    def merid(r):
        if r < 0:
            return hr[0, 2 + r, 1, 64:].astype(F32)
        if r >= clon:
            return hr[1, r - clon, 1, 64:].astype(F32)
        return wd_ref[pl.ds(64 * clon + r, 64, stride=clon), :]

    def rim_of(r):
        return (0, clon - 1) if r < 0 else (2, 0) if r >= clon else (1, r)

    def advance(r, get, rim):
        slot, j = rim_of(r)
        v = merid(r)
        v_s, v_n = shifted(v, tt[slot, 64:, :], 56 + j, 32 + j)
        q = get(r)
        south, north = shifted(q, rim, 24 + j, j)
        return step(
            q, get(r - 1), get(r + 1), south, north,
            zonal(r - 1), zonal(r), zonal(r + 1), v_s, v, v_n,
        )

    for has, side in ((has_low, 0), (has_high, 1)):
        @pl.when(has)
        def _(side=side):
            for d in (-1, 0, 1):
                pltpu.make_async_copy(
                    rp.at[side, 1 + d], rp.at[side, 1 + d], pr_sem.at[side, 1 + d]
                ).wait()

        @pl.when(jnp.logical_not(has))
        def _(side=side):
            rp[side] = jnp.zeros(rp.shape[1:], BF16)

    from_low = lax.rem(lane, 32) >= 16
    for d in range(3):
        tt[d] = jnp.where(from_low, rp[0, d].astype(F32), rp[1, d].astype(F32))

    first, last = lax.rem(lane, 8) == 0, lax.rem(lane, 8) == 7
    near = lax.rem(lane, 32) < 8
    mid = tt[1]
    edge = {
        "c": mid,
        "w": jnp.where(first, pltpu.roll(tt[0], 121, 1), pltpu.roll(mid, 1, 1)),
        "e": jnp.where(last, pltpu.roll(tt[2], 7, 1), pltpu.roll(mid, 127, 1)),
        "s": jnp.where(near, pltpu.roll(acc, 104, 1), pltpu.roll(mid, 8, 1)),
        "n": jnp.where(near, pltpu.roll(mid, 120, 1), pltpu.roll(acc, 24, 1)),
    }
    wind = {key: pltpu.roll(value, 96, 1) for key, value in edge.items()}
    outer = step(
        edge["c"], edge["w"], edge["e"], edge["s"], edge["n"],
        wind["w"][:64], wind["c"][:64], wind["e"][:64],
        wind["s"][64:], wind["c"][64:], wind["n"][64:],
    )
    outside = jnp.where(lane >= 16, a, nlat - 1 - a) > 0
    h1[...] = jnp.where(outside, outer, 0.0)

    forward(*firsts[0])
    inner = list(range(1, clon - 1))
    for r in inner:
        q1[r + 1] = advance(r, field, tt[1])
    for item in firsts[1:2]:
        forward(*item)
    for copy in halos:
        copy.wait_recv()
    for r in (-1, 0, clon - 1, clon):
        q1[r + 1] = advance(r, field, tt[rim_of(r)[0]])

    def x_copy(j):
        return pltpu.make_async_remote_copy(
            src_ref=xbuf.at[l, j], dst_ref=xbuf.at[l, j],
            send_sem=xs_sem.at[j], recv_sem=xr_sem.at[j],
            device_id={"lev": 1 - l}, device_id_type=MESH,
        )

    for r in range(clon):
        new = advance(r, lambda k: q1[k + 1], h1[...])
        st[r] = new
        xbuf[l, r] = new.T.astype(BF16)
        x_copy(r).start()
        if r == 1:
            for item in firsts[2:]:
                forward(*item)

    for copy in seconds:
        copy.wait_recv()
    local[2].wait()
    local[3].wait()

    half = clon // 2

    def y_copy(g):
        return pltpu.make_async_remote_copy(
            src_ref=pbuf.at[1 - l, pl.ds(g * half, half)], dst_ref=rbuf.at[pl.ds(g * half, half)],
            send_sem=ys_sem.at[g], recv_sem=yr_sem.at[g],
            device_id={"lev": 1 - l}, device_id_type=MESH,
        )

    hid = bi_ref.shape[1]
    for j in range(clon):
        x_copy(j).wait_recv()
    classes = [sc_ref[0, j] for j in range(clon)]
    for g in range(2):
        group = range(g * half, (g + 1) * half)
        hidden = []
        for j in group:
            x = jnp.concatenate([xbuf[0, j], xbuf[1, j]], axis=1)
            pre = jnp.dot(x, wi_all[classes[j]], preferred_element_type=F32)
            pre = pre + bias[classes[j]][0:1, :hid].astype(F32)
            hidden.append((pre * jax.nn.sigmoid(pre)).astype(BF16))
        for j, value in zip(group, hidden):
            part = jnp.dot(value, wo_all[classes[j]], preferred_element_type=F32).astype(BF16)
            pbuf[0, j] = part[:, :128]
            pbuf[1, j] = part[:, 128:]
        y_copy(g).start()

    for g in range(2):
        y_copy(g).wait_recv()
        for j in range(g * half, (g + 1) * half):
            total = pbuf[l, j].astype(F32) + rbuf[j].astype(F32)
            tend = (total + bias[classes[j]][0:1, hid:].astype(F32)).astype(BF16).astype(F32)
            out_ref[pl.ds(j, 128, stride=clon), :] = st[j] + 0.5 * tend.T

    for copy in halos:
        copy.wait_send()
    for has, side in ((has_low, 1), (has_high, 0)):
        @pl.when(has)
        def _(side=side):
            for d in (0, 1, -1):
                pack_copy(side, d).wait_send()
    for _, trio in firsts:
        for copy in trio:
            copy.wait_send()
    for copy in seconds:
        copy.wait_send()

    @pl.loop(0, clon)
    def _(j):
        x_copy(j).wait_send()

    for g in range(2):
        y_copy(g).wait_send()


def shards(sizes, tracers, winds, surface_class, w_in, b_in, w_out, b_out):
    fields, levb, clon, clat = tracers.shape
    nband, nlon, nlat = sizes
    rows = fields * levb
    flat = (rows * clon, clat)
    members = nband * 2
    vmem = pl.BlockSpec(memory_space=pltpu.VMEM)
    smem = pl.BlockSpec(memory_space=pltpu.SMEM)
    hbm = pl.BlockSpec(memory_space=pltpu.HBM)
    dma = pltpu.SemaphoreType.DMA
    new = pl.pallas_call(
        functools.partial(kernel, sizes),
        out_shape=jax.ShapeDtypeStruct(flat, F32),
        in_specs=[hbm, hbm, smem, hbm, vmem, hbm, vmem],
        out_specs=vmem,
        scratch_shapes=[
            pltpu.VMEM(flat, F32),
            pltpu.VMEM(flat, F32),
            pltpu.VMEM((4, 2, rows, clat), BF16),
            pltpu.VMEM((2, 2, 2, rows, clat), BF16),
            pltpu.VMEM((rows, clat), BF16),
            pltpu.VMEM((2, 3, rows, clat), BF16),
            pltpu.VMEM((3, rows, clat), F32),
            pltpu.VMEM((clon + 2, rows, clat), F32),
            pltpu.VMEM((rows, clat), F32),
            pltpu.VMEM((clon, rows, clat), F32),
            pltpu.VMEM((2, clon, clat, rows), BF16),
            pltpu.VMEM((2, clon, clat, rows), BF16),
            pltpu.VMEM((clon, clat, rows), BF16),
            pltpu.VMEM((nlon,) + w_in.shape[1:], BF16),
            pltpu.VMEM((nlon,) + w_out.shape[1:], BF16),
            pltpu.VMEM((nlon, 16, b_in.shape[1] + b_out.shape[1]), BF16),
            dma((2,)), dma((2,)), dma((2, 3)), dma((2, 3)), dma((4,)),
            dma((3, nlon)), dma((3, nlon)), dma((2, nlon, members)), dma((2, nlon, members)),
            dma((clon,)), dma((clon,)), dma((2,)), dma((2,)),
        ],
        compiler_params=pltpu.CompilerParams(
            collective_id=0, has_side_effects=True, vmem_limit_bytes=63 * 1024 * 1024
        ),
    )(tracers.reshape(flat), winds.reshape(flat), surface_class.reshape(1, clon), w_in, b_in, w_out, b_out)
    return new.reshape(tracers.shape)


def solution(mesh):
    placed = (
        P(None, "lev", "lon", ("band", "lat")),
        P(None, "lev", "lon", ("band", "lat")),
        P(("band", "lat"), "lon", None),
        P("lon", None, "lev"),
        P("lon", "lev"),
        P("lon", "lev", None),
        P("lon", "lev"),
    )
    sizes = tuple(mesh.shape[name] for name in ("band", "lon", "lat"))
    return jax.shard_map(
        functools.partial(shards, sizes),
        mesh=mesh,
        in_specs=placed,
        out_specs=P(None, "lev", "lon", ("band", "lat")),
        check_vma=False,
    )
```

```python
import functools

import jax
import jax.numpy as jnp
from jax import lax
from jax.experimental import pallas as pl
from jax.experimental.pallas import tpu as pltpu
from jax.sharding import PartitionSpec as P

MESH = pl.DeviceIdType.MESH
F32 = jnp.float32
BF16 = jnp.bfloat16


def step(q, west, east, south, north, u_w, u, u_e, v_s, v, v_n):
    levels = u.shape[0]
    face_e = 0.5 * (u + u_e)
    face_w = 0.5 * (u_w + u)
    face_n = 0.5 * (v + v_n)
    face_s = 0.5 * (v_s + v)
    e_pos, e_neg = jnp.maximum(face_e, 0.0), jnp.minimum(face_e, 0.0)
    w_pos, w_neg = jnp.maximum(face_w, 0.0), jnp.minimum(face_w, 0.0)
    n_pos, n_neg = jnp.maximum(face_n, 0.0), jnp.minimum(face_n, 0.0)
    s_pos, s_neg = jnp.maximum(face_s, 0.0), jnp.minimum(face_s, 0.0)
    parts = []
    for f in range(q.shape[0] // levels):
        cut = slice(f * levels, (f + 1) * levels)
        c = q[cut]
        div_x = (e_pos * c + e_neg * east[cut]) - (w_pos * west[cut] + w_neg * c)
        div_y = (n_pos * c + n_neg * north[cut]) - (s_pos * south[cut] + s_neg * c)
        parts.append((c - div_x) - div_y)
    return jnp.concatenate(parts, axis=0)


def kernel(
    sizes,
    tr_hbm, wd_hbm, sc_ref, wi_ref, bi_ref, wo_ref, bo_ref,
    out_ref,
    tr_ref, wd_ref, hs, hr, pack, rp, tt, q1, h1, st, xbuf, pbuf, rbuf, wi_all, wo_all, bias,
    hs_sem, hr_sem, ps_sem, pr_sem, loc_sem, a_send, a_recv, b_send, b_recv,
    xs_sem, xr_sem, ys_sem, yr_sem,
):
    nband, nlon, nlat = sizes
    b, z, a, l = (lax.axis_index(n) for n in ("band", "lon", "lat", "lev"))
    clon = out_ref.shape[0] // 128
    rows_i = wi_ref.shape[1] // (nband * 2)
    rows_o = wo_ref.shape[1] // (nband * 2)
    p = b * 2 + lax.rem(a, 2)
    pair = a - lax.rem(a, 2)
    has_low, has_high = a > 0, a < nlat - 1

    def lon_at(d):
        return lax.rem(z + d + nlon, nlon)

    def peer_of(k):
        other = lax.rem(p + k, nband * 2)
        return {"band": other // 2, "lat": pair + lax.rem(other, 2)}, other

    local = [
        pltpu.make_async_copy(tr_hbm, tr_ref, loc_sem.at[2]),
        pltpu.make_async_copy(wd_hbm, wd_ref, loc_sem.at[3]),
        pltpu.make_async_copy(wi_ref.at[0], wi_all.at[z], loc_sem.at[0]),
        pltpu.make_async_copy(wo_ref.at[0], wo_all.at[z], loc_sem.at[1]),
    ]
    for copy in local:
        copy.start()

    barrier = pltpu.get_barrier_semaphore()
    for d in range(1, nlon):
        pl.semaphore_signal(barrier, inc=1, device_id={"lon": lon_at(d)}, device_id_type=MESH)
    for k in range(1, nband * 2):
        pl.semaphore_signal(barrier, inc=1, device_id=peer_of(k)[0], device_id_type=MESH)
    pl.semaphore_signal(barrier, inc=1, device_id={"lev": 1 - l}, device_id_type=MESH)
    for has, da in ((has_low, -1), (has_high, 1)):
        @pl.when(has)
        def _(da=da):
            for d in (-1, 0, 1):
                pl.semaphore_signal(
                    barrier, inc=1, device_id={"lat": a + da, "lon": lon_at(d)}, device_id_type=MESH
                )

    def own(ref, j):
        return ref[pl.ds(j, 128, stride=clon), :]

    local[0].wait()
    local[1].wait()
    for slot, j in enumerate((0, 1, clon - 2, clon - 1)):
        hs[slot, 0] = own(tr_ref, j).astype(BF16)
        hs[slot, 1] = own(wd_ref, j).astype(BF16)
    bias[z, :, : bi_ref.shape[1]] = jnp.broadcast_to(
        bi_ref[...].astype(F32), (16, bi_ref.shape[1])
    ).astype(BF16)
    bias[z, :, bi_ref.shape[1]:] = jnp.broadcast_to(
        bo_ref[...].astype(F32), (16, bo_ref.shape[1])
    ).astype(BF16)

    sides = (a + nlat - 1) // nlat + (2 * nlat - 2 - a) // nlat
    pl.semaphore_wait(barrier, nlon - 1 + nband * 2 - 1 + 1 + 3 * sides)

    halos = []
    for side, d in ((0, 1), (1, -1)):
        first = 2 if d == 1 else 0
        halos.append(pltpu.make_async_remote_copy(
            src_ref=hs.at[pl.ds(first, 2)], dst_ref=hr.at[side],
            send_sem=hs_sem.at[side], recv_sem=hr_sem.at[side],
            device_id={"lon": lon_at(d)}, device_id_type=MESH,
        ))
        halos[-1].start()

    lane = lax.broadcasted_iota(jnp.int32, (128, 128), 1)
    acc = jnp.zeros((128, 128), F32)
    for base, ref in ((0, tr_ref), (32, wd_ref)):
        for j in range(clon):
            x = own(ref, j)
            for g, col in enumerate((0, 1, 126, 127)):
                place = base + g * 8 + j
                acc = jnp.where(lane == place, pltpu.roll(x, (place - col) % 128, 1), acc)
    pack[...] = acc.astype(BF16)

    def pack_copy(side, d):
        return pltpu.make_async_remote_copy(
            src_ref=pack, dst_ref=rp.at[side, 1 - d],
            send_sem=ps_sem.at[side, 1 - d], recv_sem=pr_sem.at[side, 1 - d],
            device_id={"lat": a + (1 if side == 0 else -1), "lon": lon_at(d)}, device_id_type=MESH,
        )

    for has, side in ((has_low, 1), (has_high, 0)):
        @pl.when(has)
        def _(side=side):
            for d in (0, 1, -1):
                pack_copy(side, d).start()

    cut_i, cut_o = pl.ds(p * rows_i, rows_i), pl.ds(p * rows_o, rows_o)
    order = sorted(range(1, nlon), key=lambda d: min(d, nlon - d))
    firsts = []
    for d in order:
        trio = []
        for kind, (src, dst) in enumerate((
            (wi_ref.at[0, cut_i], wi_all.at[z, cut_i]),
            (wo_ref.at[0, cut_o], wo_all.at[z, cut_o]),
            (bias.at[z], bias.at[z]),
        )):
            trio.append(pltpu.make_async_remote_copy(
                src_ref=src, dst_ref=dst,
                send_sem=a_send.at[kind, d], recv_sem=a_recv.at[kind, d],
                device_id={"lon": lon_at(d)}, device_id_type=MESH,
            ))
            trio[-1].start()
        firsts.append((d, trio))

    seconds = []

    def forward(d, trio):
        for copy in trio:
            copy.wait_recv()
        c = lon_at(-d)
        for k in range(1, nband * 2):
            for kind, (buf, cut) in enumerate(((wi_all, cut_i), (wo_all, cut_o))):
                copy = pltpu.make_async_remote_copy(
                    src_ref=buf.at[c, cut], dst_ref=buf.at[c, cut],
                    send_sem=b_send.at[kind, d, k], recv_sem=b_recv.at[kind, d, k],
                    device_id=peer_of(k)[0], device_id_type=MESH,
                )
                copy.start()
                seconds.append(copy)

    def shifted(x, rim, low_lane, high_lane):
        ln = lane[: x.shape[0]]
        south = jnp.where(ln == 0, pltpu.roll(rim, (128 - low_lane) % 128, 1), pltpu.roll(x, 1, 1))
        north = jnp.where(
            ln == 127, pltpu.roll(rim, (127 - high_lane) % 128, 1), pltpu.roll(x, 127, 1)
        )
        return south, north

    def field(r):
        if r < 0:
            return hr[0, 2 + r, 0].astype(F32)
        if r >= clon:
            return hr[1, r - clon, 0].astype(F32)
        return own(tr_ref, r)

    def zonal(r):
        if r < 0:
            return hr[0, 2 + r, 1, :64].astype(F32)
        if r >= clon:
            return hr[1, r - clon, 1, :64].astype(F32)
        return wd_ref[pl.ds(r, 64, stride=clon), :]

    def merid(r):
        if r < 0:
            return hr[0, 2 + r, 1, 64:].astype(F32)
        if r >= clon:
            return hr[1, r - clon, 1, 64:].astype(F32)
        return wd_ref[pl.ds(64 * clon + r, 64, stride=clon), :]

    def rim_of(r):
        return (0, clon - 1) if r < 0 else (2, 0) if r >= clon else (1, r)

    def advance(r, get, rim):
        slot, j = rim_of(r)
        v = merid(r)
        v_s, v_n = shifted(v, tt[slot, 64:, :], 56 + j, 32 + j)
        q = get(r)
        south, north = shifted(q, rim, 24 + j, j)
        return step(
            q, get(r - 1), get(r + 1), south, north,
            zonal(r - 1), zonal(r), zonal(r + 1), v_s, v, v_n,
        )

    for has, side in ((has_low, 0), (has_high, 1)):
        @pl.when(has)
        def _(side=side):
            for d in (-1, 0, 1):
                pltpu.make_async_copy(
                    rp.at[side, 1 + d], rp.at[side, 1 + d], pr_sem.at[side, 1 + d]
                ).wait()

        @pl.when(jnp.logical_not(has))
        def _(side=side):
            rp[side] = jnp.zeros(rp.shape[1:], BF16)

    from_low = lax.rem(lane, 32) >= 16
    for d in range(3):
        tt[d] = jnp.where(from_low, rp[0, d].astype(F32), rp[1, d].astype(F32))

    first, last = lax.rem(lane, 8) == 0, lax.rem(lane, 8) == 7
    near = lax.rem(lane, 32) < 8
    mid = tt[1]
    edge = {
        "c": mid,
        "w": jnp.where(first, pltpu.roll(tt[0], 121, 1), pltpu.roll(mid, 1, 1)),
        "e": jnp.where(last, pltpu.roll(tt[2], 7, 1), pltpu.roll(mid, 127, 1)),
        "s": jnp.where(near, pltpu.roll(acc, 104, 1), pltpu.roll(mid, 8, 1)),
        "n": jnp.where(near, pltpu.roll(mid, 120, 1), pltpu.roll(acc, 24, 1)),
    }
    wind = {key: pltpu.roll(value, 96, 1) for key, value in edge.items()}
    outer = step(
        edge["c"], edge["w"], edge["e"], edge["s"], edge["n"],
        wind["w"][:64], wind["c"][:64], wind["e"][:64],
        wind["s"][64:], wind["c"][64:], wind["n"][64:],
    )
    outside = jnp.where(lane >= 16, a, nlat - 1 - a) > 0
    h1[...] = jnp.where(outside, outer, 0.0)

    forward(*firsts[0])
    inner = list(range(1, clon - 1))
    for r in inner:
        q1[r + 1] = advance(r, field, tt[1])
    for item in firsts[1:2]:
        forward(*item)
    for copy in halos:
        copy.wait_recv()
    for r in (-1, 0, clon - 1, clon):
        q1[r + 1] = advance(r, field, tt[rim_of(r)[0]])

    def x_copy(j):
        return pltpu.make_async_remote_copy(
            src_ref=xbuf.at[l, j], dst_ref=xbuf.at[l, j],
            send_sem=xs_sem.at[j], recv_sem=xr_sem.at[j],
            device_id={"lev": 1 - l}, device_id_type=MESH,
        )

    for r in range(clon):
        new = advance(r, lambda k: q1[k + 1], h1[...])
        st[r] = new
        xbuf[l, r] = new.T.astype(BF16)
        x_copy(r).start()
        if r == 1:
            for item in firsts[2:]:
                forward(*item)

    for copy in seconds:
        copy.wait_recv()
    local[2].wait()
    local[3].wait()

    half = clon // 2

    def y_copy(g):
        return pltpu.make_async_remote_copy(
            src_ref=pbuf.at[1 - l, pl.ds(g * half, half)], dst_ref=rbuf.at[pl.ds(g * half, half)],
            send_sem=ys_sem.at[g], recv_sem=yr_sem.at[g],
            device_id={"lev": 1 - l}, device_id_type=MESH,
        )

    hid = bi_ref.shape[1]
    for j in range(clon):
        x_copy(j).wait_recv()
    classes = [sc_ref[0, j] for j in range(clon)]
    for g in range(2):
        group = range(g * half, (g + 1) * half)
        hidden = []
        for j in group:
            x = jnp.concatenate([xbuf[0, j], xbuf[1, j]], axis=1)
            pre = jnp.dot(x, wi_all[classes[j]], preferred_element_type=F32)
            pre = pre + bias[classes[j]][0:1, :hid].astype(F32)
            hidden.append((pre * jax.nn.sigmoid(pre)).astype(BF16))
        for j, value in zip(group, hidden):
            part = jnp.dot(value, wo_all[classes[j]], preferred_element_type=F32).astype(BF16)
            pbuf[0, j] = part[:, :128]
            pbuf[1, j] = part[:, 128:]
        y_copy(g).start()

    for g in range(2):
        y_copy(g).wait_recv()
        for j in range(g * half, (g + 1) * half):
            total = pbuf[l, j].astype(F32) + rbuf[j].astype(F32)
            tend = (total + bias[classes[j]][0:1, hid:].astype(F32)).astype(BF16).astype(F32)
            out_ref[pl.ds(j, 128, stride=clon), :] = st[j] + 0.5 * tend.T

    for copy in halos:
        copy.wait_send()
    for has, side in ((has_low, 1), (has_high, 0)):
        @pl.when(has)
        def _(side=side):
            for d in (0, 1, -1):
                pack_copy(side, d).wait_send()
    for _, trio in firsts:
        for copy in trio:
            copy.wait_send()
    for copy in seconds:
        copy.wait_send()

    @pl.loop(0, clon)
    def _(j):
        x_copy(j).wait_send()

    for g in range(2):
        y_copy(g).wait_send()


def shards(sizes, tracers, winds, surface_class, w_in, b_in, w_out, b_out):
    fields, levb, clon, clat = tracers.shape
    nband, nlon, nlat = sizes
    rows = fields * levb
    flat = (rows * clon, clat)
    members = nband * 2
    vmem = pl.BlockSpec(memory_space=pltpu.VMEM)
    smem = pl.BlockSpec(memory_space=pltpu.SMEM)
    hbm = pl.BlockSpec(memory_space=pltpu.HBM)
    dma = pltpu.SemaphoreType.DMA
    new = pl.pallas_call(
        functools.partial(kernel, sizes),
        out_shape=jax.ShapeDtypeStruct(flat, F32),
        in_specs=[hbm, hbm, smem, hbm, vmem, hbm, vmem],
        out_specs=vmem,
        scratch_shapes=[
            pltpu.VMEM(flat, F32),
            pltpu.VMEM(flat, F32),
            pltpu.VMEM((4, 2, rows, clat), BF16),
            pltpu.VMEM((2, 2, 2, rows, clat), BF16),
            pltpu.VMEM((rows, clat), BF16),
            pltpu.VMEM((2, 3, rows, clat), BF16),
            pltpu.VMEM((3, rows, clat), F32),
            pltpu.VMEM((clon + 2, rows, clat), F32),
            pltpu.VMEM((rows, clat), F32),
            pltpu.VMEM((clon, rows, clat), F32),
            pltpu.VMEM((2, clon, clat, rows), BF16),
            pltpu.VMEM((2, clon, clat, rows), BF16),
            pltpu.VMEM((clon, clat, rows), BF16),
            pltpu.VMEM((nlon,) + w_in.shape[1:], BF16),
            pltpu.VMEM((nlon,) + w_out.shape[1:], BF16),
            pltpu.VMEM((nlon, 16, b_in.shape[1] + b_out.shape[1]), BF16),
            dma((2,)), dma((2,)), dma((2, 3)), dma((2, 3)), dma((4,)),
            dma((3, nlon)), dma((3, nlon)), dma((2, nlon, members)), dma((2, nlon, members)),
            dma((clon,)), dma((clon,)), dma((2,)), dma((2,)),
        ],
        compiler_params=pltpu.CompilerParams(
            collective_id=0, has_side_effects=True, vmem_limit_bytes=63 * 1024 * 1024
        ),
    )(tracers.reshape(flat), winds.reshape(flat), surface_class.reshape(1, clon), w_in, b_in, w_out, b_out)
    return new.reshape(tracers.shape)


def solution(mesh):
    placed = (
        P(None, "lev", "lon", ("band", "lat")),
        P(None, "lev", "lon", ("band", "lat")),
        P(("band", "lat"), "lon", None),
        P("lon", None, "lev"),
        P("lon", "lev"),
        P("lon", "lev", None),
        P("lon", "lev"),
    )
    sizes = tuple(mesh.shape[name] for name in ("band", "lon", "lat"))
    return jax.shard_map(
        functools.partial(shards, sizes),
        mesh=mesh,
        in_specs=placed,
        out_specs=P(None, "lev", "lon", ("band", "lat")),
        check_vma=False,
    )
```

```python
import functools

import jax
import jax.numpy as jnp
from jax import lax
from jax.experimental import pallas as pl
from jax.experimental.pallas import tpu as pltpu
from jax.sharding import PartitionSpec as P

MESH = pl.DeviceIdType.MESH
F32 = jnp.float32
BF16 = jnp.bfloat16


def step(q, west, east, south, north, u_w, u, u_e, v_s, v, v_n):
    levels = u.shape[0]
    face_e = 0.5 * (u + u_e)
    face_w = 0.5 * (u_w + u)
    face_n = 0.5 * (v + v_n)
    face_s = 0.5 * (v_s + v)
    e_pos, e_neg = jnp.maximum(face_e, 0.0), jnp.minimum(face_e, 0.0)
    w_pos, w_neg = jnp.maximum(face_w, 0.0), jnp.minimum(face_w, 0.0)
    n_pos, n_neg = jnp.maximum(face_n, 0.0), jnp.minimum(face_n, 0.0)
    s_pos, s_neg = jnp.maximum(face_s, 0.0), jnp.minimum(face_s, 0.0)
    parts = []
    for f in range(q.shape[0] // levels):
        cut = slice(f * levels, (f + 1) * levels)
        c = q[cut]
        div_x = (e_pos * c + e_neg * east[cut]) - (w_pos * west[cut] + w_neg * c)
        div_y = (n_pos * c + n_neg * north[cut]) - (s_pos * south[cut] + s_neg * c)
        parts.append((c - div_x) - div_y)
    return jnp.concatenate(parts, axis=0)


def kernel(
    sizes,
    tr_hbm, wd_hbm, sc_ref, wi_ref, bi_ref, wo_ref, bo_ref,
    out_ref,
    tr_ref, wd_ref, hs, hr, pack, rp, tt, q1, h1, st, xbuf, pbuf, rbuf, wi_all, wo_all, bias,
    hs_sem, hr_sem, ps_sem, pr_sem, loc_sem, a_send, a_recv, b_send, b_recv,
    xs_sem, xr_sem, ys_sem, yr_sem,
):
    nband, nlon, nlat = sizes
    b, z, a, l = (lax.axis_index(n) for n in ("band", "lon", "lat", "lev"))
    clon = out_ref.shape[0] // 128
    rows_i = wi_ref.shape[1] // (nband * 2)
    rows_o = wo_ref.shape[1] // (nband * 2)
    p = b * 2 + lax.rem(a, 2)
    pair = a - lax.rem(a, 2)
    has_low, has_high = a > 0, a < nlat - 1

    def lon_at(d):
        return lax.rem(z + d + nlon, nlon)

    def peer_of(k):
        other = lax.rem(p + k, nband * 2)
        return {"band": other // 2, "lat": pair + lax.rem(other, 2)}, other

    local = [
        pltpu.make_async_copy(tr_hbm, tr_ref, loc_sem.at[2]),
        pltpu.make_async_copy(wd_hbm, wd_ref, loc_sem.at[3]),
        pltpu.make_async_copy(wi_ref.at[0], wi_all.at[z], loc_sem.at[0]),
        pltpu.make_async_copy(wo_ref.at[0], wo_all.at[z], loc_sem.at[1]),
    ]
    for copy in local:
        copy.start()

    barrier = pltpu.get_barrier_semaphore()
    for d in range(1, nlon):
        pl.semaphore_signal(barrier, inc=1, device_id={"lon": lon_at(d)}, device_id_type=MESH)
    for k in range(1, nband * 2):
        pl.semaphore_signal(barrier, inc=1, device_id=peer_of(k)[0], device_id_type=MESH)
    pl.semaphore_signal(barrier, inc=1, device_id={"lev": 1 - l}, device_id_type=MESH)
    for has, da in ((has_low, -1), (has_high, 1)):
        @pl.when(has)
        def _(da=da):
            for d in (-1, 0, 1):
                pl.semaphore_signal(
                    barrier, inc=1, device_id={"lat": a + da, "lon": lon_at(d)}, device_id_type=MESH
                )

    def own(ref, j):
        return ref[pl.ds(j, 128, stride=clon), :]

    local[0].wait()
    local[1].wait()
    for slot, j in enumerate((0, 1, clon - 2, clon - 1)):
        hs[slot, 0] = own(tr_ref, j).astype(BF16)
        hs[slot, 1] = own(wd_ref, j).astype(BF16)
    bias[z, :, : bi_ref.shape[1]] = jnp.broadcast_to(
        bi_ref[...].astype(F32), (16, bi_ref.shape[1])
    ).astype(BF16)
    bias[z, :, bi_ref.shape[1]:] = jnp.broadcast_to(
        bo_ref[...].astype(F32), (16, bo_ref.shape[1])
    ).astype(BF16)

    sides = (a + nlat - 1) // nlat + (2 * nlat - 2 - a) // nlat
    pl.semaphore_wait(barrier, nlon - 1 + nband * 2 - 1 + 1 + 3 * sides)

    halos = []
    for side, d in ((0, 1), (1, -1)):
        first = 2 if d == 1 else 0
        halos.append(pltpu.make_async_remote_copy(
            src_ref=hs.at[pl.ds(first, 2)], dst_ref=hr.at[side],
            send_sem=hs_sem.at[side], recv_sem=hr_sem.at[side],
            device_id={"lon": lon_at(d)}, device_id_type=MESH,
        ))
        halos[-1].start()

    lane = lax.broadcasted_iota(jnp.int32, (128, 128), 1)
    acc = jnp.zeros((128, 128), F32)
    for base, ref in ((0, tr_ref), (32, wd_ref)):
        for j in range(clon):
            x = own(ref, j)
            for g, col in enumerate((0, 1, 126, 127)):
                place = base + g * 8 + j
                acc = jnp.where(lane == place, pltpu.roll(x, (place - col) % 128, 1), acc)
    pack[...] = acc.astype(BF16)

    def pack_copy(side, d):
        return pltpu.make_async_remote_copy(
            src_ref=pack, dst_ref=rp.at[side, 1 - d],
            send_sem=ps_sem.at[side, 1 - d], recv_sem=pr_sem.at[side, 1 - d],
            device_id={"lat": a + (1 if side == 0 else -1), "lon": lon_at(d)}, device_id_type=MESH,
        )

    for has, side in ((has_low, 1), (has_high, 0)):
        @pl.when(has)
        def _(side=side):
            for d in (0, 1, -1):
                pack_copy(side, d).start()

    cut_i, cut_o = pl.ds(p * rows_i, rows_i), pl.ds(p * rows_o, rows_o)
    order = sorted(range(1, nlon), key=lambda d: min(d, nlon - d))
    firsts = []
    for d in order:
        trio = []
        for kind, (src, dst) in enumerate((
            (wi_ref.at[0, cut_i], wi_all.at[z, cut_i]),
            (wo_ref.at[0, cut_o], wo_all.at[z, cut_o]),
            (bias.at[z], bias.at[z]),
        )):
            trio.append(pltpu.make_async_remote_copy(
                src_ref=src, dst_ref=dst,
                send_sem=a_send.at[kind, d], recv_sem=a_recv.at[kind, d],
                device_id={"lon": lon_at(d)}, device_id_type=MESH,
            ))
            trio[-1].start()
        firsts.append((d, trio))

    seconds = []

    def forward(d, trio):
        for copy in trio:
            copy.wait_recv()
        c = lon_at(-d)
        for k in range(1, nband * 2):
            for kind, (buf, cut) in enumerate(((wi_all, cut_i), (wo_all, cut_o))):
                copy = pltpu.make_async_remote_copy(
                    src_ref=buf.at[c, cut], dst_ref=buf.at[c, cut],
                    send_sem=b_send.at[kind, d, k], recv_sem=b_recv.at[kind, d, k],
                    device_id=peer_of(k)[0], device_id_type=MESH,
                )
                copy.start()
                seconds.append(copy)

    def shifted(x, rim, low_lane, high_lane):
        ln = lane[: x.shape[0]]
        south = jnp.where(ln == 0, pltpu.roll(rim, (128 - low_lane) % 128, 1), pltpu.roll(x, 1, 1))
        north = jnp.where(
            ln == 127, pltpu.roll(rim, (127 - high_lane) % 128, 1), pltpu.roll(x, 127, 1)
        )
        return south, north

    def field(r):
        if r < 0:
            return hr[0, 2 + r, 0].astype(F32)
        if r >= clon:
            return hr[1, r - clon, 0].astype(F32)
        return own(tr_ref, r)

    def zonal(r):
        if r < 0:
            return hr[0, 2 + r, 1, :64].astype(F32)
        if r >= clon:
            return hr[1, r - clon, 1, :64].astype(F32)
        return wd_ref[pl.ds(r, 64, stride=clon), :]

    def merid(r):
        if r < 0:
            return hr[0, 2 + r, 1, 64:].astype(F32)
        if r >= clon:
            return hr[1, r - clon, 1, 64:].astype(F32)
        return wd_ref[pl.ds(64 * clon + r, 64, stride=clon), :]

    def rim_of(r):
        return (0, clon - 1) if r < 0 else (2, 0) if r >= clon else (1, r)

    def advance(r, get, rim):
        slot, j = rim_of(r)
        v = merid(r)
        v_s, v_n = shifted(v, tt[slot, 64:, :], 56 + j, 32 + j)
        q = get(r)
        south, north = shifted(q, rim, 24 + j, j)
        return step(
            q, get(r - 1), get(r + 1), south, north,
            zonal(r - 1), zonal(r), zonal(r + 1), v_s, v, v_n,
        )

    for has, side in ((has_low, 0), (has_high, 1)):
        @pl.when(has)
        def _(side=side):
            for d in (-1, 0, 1):
                pltpu.make_async_copy(
                    rp.at[side, 1 + d], rp.at[side, 1 + d], pr_sem.at[side, 1 + d]
                ).wait()

        @pl.when(jnp.logical_not(has))
        def _(side=side):
            rp[side] = jnp.zeros(rp.shape[1:], BF16)

    from_low = lax.rem(lane, 32) >= 16
    for d in range(3):
        tt[d] = jnp.where(from_low, rp[0, d].astype(F32), rp[1, d].astype(F32))

    first, last = lax.rem(lane, 8) == 0, lax.rem(lane, 8) == 7
    near = lax.rem(lane, 32) < 8
    mid = tt[1]
    edge = {
        "c": mid,
        "w": jnp.where(first, pltpu.roll(tt[0], 121, 1), pltpu.roll(mid, 1, 1)),
        "e": jnp.where(last, pltpu.roll(tt[2], 7, 1), pltpu.roll(mid, 127, 1)),
        "s": jnp.where(near, pltpu.roll(acc, 104, 1), pltpu.roll(mid, 8, 1)),
        "n": jnp.where(near, pltpu.roll(mid, 120, 1), pltpu.roll(acc, 24, 1)),
    }
    wind = {key: pltpu.roll(value, 96, 1) for key, value in edge.items()}
    outer = step(
        edge["c"], edge["w"], edge["e"], edge["s"], edge["n"],
        wind["w"][:64], wind["c"][:64], wind["e"][:64],
        wind["s"][64:], wind["c"][64:], wind["n"][64:],
    )
    outside = jnp.where(lane >= 16, a, nlat - 1 - a) > 0
    h1[...] = jnp.where(outside, outer, 0.0)

    forward(*firsts[0])
    inner = list(range(1, clon - 1))
    for r in inner:
        q1[r + 1] = advance(r, field, tt[1])
    for item in firsts[1:2]:
        forward(*item)
    for copy in halos:
        copy.wait_recv()
    for r in (-1, 0, clon - 1, clon):
        q1[r + 1] = advance(r, field, tt[rim_of(r)[0]])

    def x_copy(j):
        return pltpu.make_async_remote_copy(
            src_ref=xbuf.at[l, j], dst_ref=xbuf.at[l, j],
            send_sem=xs_sem.at[j], recv_sem=xr_sem.at[j],
            device_id={"lev": 1 - l}, device_id_type=MESH,
        )

    for r in range(clon):
        new = advance(r, lambda k: q1[k + 1], h1[...])
        st[r] = new
        xbuf[l, r] = new.T.astype(BF16)
        x_copy(r).start()
        if r == clon - 1:
            for item in firsts[2:]:
                forward(*item)

    for copy in seconds:
        copy.wait_recv()
    local[2].wait()
    local[3].wait()

    half = clon // 2

    def y_copy(g):
        return pltpu.make_async_remote_copy(
            src_ref=pbuf.at[1 - l, pl.ds(g * half, half)], dst_ref=rbuf.at[pl.ds(g * half, half)],
            send_sem=ys_sem.at[g], recv_sem=yr_sem.at[g],
            device_id={"lev": 1 - l}, device_id_type=MESH,
        )

    hid = bi_ref.shape[1]
    for j in range(clon):
        x_copy(j).wait_recv()
    classes = [sc_ref[0, j] for j in range(clon)]
    for g in range(2):
        group = range(g * half, (g + 1) * half)
        hidden = []
        for j in group:
            x = jnp.concatenate([xbuf[0, j], xbuf[1, j]], axis=1)
            pre = jnp.dot(x, wi_all[classes[j]], preferred_element_type=F32)
            pre = pre + bias[classes[j]][0:1, :hid].astype(F32)
            hidden.append((pre * jax.nn.sigmoid(pre)).astype(BF16))
        for j, value in zip(group, hidden):
            part = jnp.dot(value, wo_all[classes[j]], preferred_element_type=F32).astype(BF16)
            pbuf[0, j] = part[:, :128]
            pbuf[1, j] = part[:, 128:]
        y_copy(g).start()

    for g in range(2):
        y_copy(g).wait_recv()
        for j in range(g * half, (g + 1) * half):
            total = pbuf[l, j].astype(F32) + rbuf[j].astype(F32)
            tend = (total + bias[classes[j]][0:1, hid:].astype(F32)).astype(BF16).astype(F32)
            out_ref[pl.ds(j, 128, stride=clon), :] = st[j] + 0.5 * tend.T

    for copy in halos:
        copy.wait_send()
    for has, side in ((has_low, 1), (has_high, 0)):
        @pl.when(has)
        def _(side=side):
            for d in (0, 1, -1):
                pack_copy(side, d).wait_send()
    for _, trio in firsts:
        for copy in trio:
            copy.wait_send()
    for copy in seconds:
        copy.wait_send()

    @pl.loop(0, clon)
    def _(j):
        x_copy(j).wait_send()

    for g in range(2):
        y_copy(g).wait_send()


def shards(sizes, tracers, winds, surface_class, w_in, b_in, w_out, b_out):
    fields, levb, clon, clat = tracers.shape
    nband, nlon, nlat = sizes
    rows = fields * levb
    flat = (rows * clon, clat)
    members = nband * 2
    vmem = pl.BlockSpec(memory_space=pltpu.VMEM)
    smem = pl.BlockSpec(memory_space=pltpu.SMEM)
    hbm = pl.BlockSpec(memory_space=pltpu.HBM)
    dma = pltpu.SemaphoreType.DMA
    new = pl.pallas_call(
        functools.partial(kernel, sizes),
        out_shape=jax.ShapeDtypeStruct(flat, F32),
        in_specs=[hbm, hbm, smem, hbm, vmem, hbm, vmem],
        out_specs=vmem,
        scratch_shapes=[
            pltpu.VMEM(flat, F32),
            pltpu.VMEM(flat, F32),
            pltpu.VMEM((4, 2, rows, clat), BF16),
            pltpu.VMEM((2, 2, 2, rows, clat), BF16),
            pltpu.VMEM((rows, clat), BF16),
            pltpu.VMEM((2, 3, rows, clat), BF16),
            pltpu.VMEM((3, rows, clat), F32),
            pltpu.VMEM((clon + 2, rows, clat), F32),
            pltpu.VMEM((rows, clat), F32),
            pltpu.VMEM((clon, rows, clat), F32),
            pltpu.VMEM((2, clon, clat, rows), BF16),
            pltpu.VMEM((2, clon, clat, rows), BF16),
            pltpu.VMEM((clon, clat, rows), BF16),
            pltpu.VMEM((nlon,) + w_in.shape[1:], BF16),
            pltpu.VMEM((nlon,) + w_out.shape[1:], BF16),
            pltpu.VMEM((nlon, 16, b_in.shape[1] + b_out.shape[1]), BF16),
            dma((2,)), dma((2,)), dma((2, 3)), dma((2, 3)), dma((4,)),
            dma((3, nlon)), dma((3, nlon)), dma((2, nlon, members)), dma((2, nlon, members)),
            dma((clon,)), dma((clon,)), dma((2,)), dma((2,)),
        ],
        compiler_params=pltpu.CompilerParams(
            collective_id=0, has_side_effects=True, vmem_limit_bytes=63 * 1024 * 1024
        ),
    )(tracers.reshape(flat), winds.reshape(flat), surface_class.reshape(1, clon), w_in, b_in, w_out, b_out)
    return new.reshape(tracers.shape)


def solution(mesh):
    placed = (
        P(None, "lev", "lon", ("band", "lat")),
        P(None, "lev", "lon", ("band", "lat")),
        P(("band", "lat"), "lon", None),
        P("lon", None, "lev"),
        P("lon", "lev"),
        P("lon", "lev", None),
        P("lon", "lev"),
    )
    sizes = tuple(mesh.shape[name] for name in ("band", "lon", "lat"))
    return jax.shard_map(
        functools.partial(shards, sizes),
        mesh=mesh,
        in_specs=placed,
        out_specs=P(None, "lev", "lon", ("band", "lat")),
        check_vma=False,
    )
```
